512 devices in a mesh: gx: 32 (over z, core), gy: 16 (over y, x).
Axes of the slice: x: 4, y: 4, z: 16, core: 2. Of those that a mesh axis runs over, the one named last changes fastest.
Arguments:
- charge_densities: float32 [2, 128, 512, 256], P(None, 'gx', 'gy'), may hold values from 0.2 to 5
- upwind_linkage: float32 [2, 2, 128, 512, 256], P(None, None, 'gx', 'gy'), may hold values from 0.1 to 1, as said below
- decay_duration: float32 [128, 512, 256], P('gx', 'gy'), may hold values from 0.3 to 3
- deposited_packets: float32 [32, 16, 32, 8, 128], P('gx', 'gy'), may hold values from 0.25 to 4
- active_packet_tally: int32 [32, 16, 32], P('gx', 'gy'), may hold values from 0 to 8, as said below
- receiving_packet_position: int32 [32, 16, 32, 8], P('gx', 'gy'), may hold values from 0 to 255
Outputs:
- updated: float32 [2, 128, 512, 256], P(None, 'gx', 'gy')
The draws below stay inside these ranges and needn't reach their ends.
Inputs may be any that keep to these rules, and one draw needn't show every extreme that they name: `upwind_linkage`: its values lie strictly between 0 and 1. active_packet_tally[s, r, d] counts the live slots, the first ones, of the blocks from tile s to tile d in row r; it is at most 8 and reaches 8 in every draw.
All inputs are finite; a program needn't handle non-finite values.
Results may differ from the reference program's by a relative error of at most 0.000071.
Values sent between devices are 32-bit elements; how exact they have to be, the bound alone decides.
A program may use at most 64 MiB of HBM per device.

```python
import math
import jax
import jax.numpy as jnp
from jax import lax

CX = 4
CY = 32
MESH_DEPTH = 256
ZB = 128
CAP = 8
MESH_WIDTH = 128
MESH_HEIGHT = 512
BLOCKS = 256
N_GX = 32
N_GY = 16


def line_rates(keys, shape, length, share):
    slow = jax.random.uniform(keys[0], shape, jnp.float32, 0.25, 0.75) / length
    fast = jnp.exp(jax.random.uniform(keys[1], shape, jnp.float32, math.log(0.025), math.log(0.6)))
    picked = jax.random.uniform(keys[2], shape, jnp.float32) < share
    return jnp.where(picked, slow, fast)


def draw_upwind_linkage(key, part):
    keys = jax.random.split(jax.random.fold_in(key, 7), 10)
    share = 0.5
    rate_x = line_rates(keys[0:3], (2, 1, MESH_HEIGHT, MESH_DEPTH), MESH_WIDTH, share)
    rate_y = line_rates(keys[3:6], (2, MESH_WIDTH, 1, MESH_DEPTH), MESH_HEIGHT, share)
    full_shape = (2, MESH_WIDTH, MESH_HEIGHT, MESH_DEPTH)
    rates = jnp.stack([jnp.broadcast_to(rate_x, full_shape), jnp.broadcast_to(rate_y, full_shape)])
    rough = jax.random.uniform(keys[6], (2, 2, MESH_WIDTH, MESH_HEIGHT, MESH_DEPTH), jnp.float32, 0.5, 2.0)
    lengths = jnp.array([MESH_WIDTH, MESH_HEIGHT], jnp.float32).reshape(2, 1, 1, 1, 1)
    struck = jax.random.uniform(keys[7], (2, 2, MESH_WIDTH, MESH_HEIGHT, MESH_DEPTH), jnp.float32) < 2.0 / lengths
    losses = jax.random.uniform(keys[8], (2, 2, MESH_WIDTH, MESH_HEIGHT, MESH_DEPTH), jnp.float32, 0.5, 0.8)
    return jnp.exp(-rates * rough) * jnp.where(struck, losses, 1.0)


def draw_active_packet_tally(key, part):
    keys = jax.random.split(jax.random.fold_in(key, 11), 4)
    entry = jax.random.randint(keys[0], (N_GX, N_GY), 0, N_GX)
    span = jax.random.randint(keys[1], (N_GX, N_GY), N_GX // 4, N_GX // 2 + 1)
    dest = jnp.arange(N_GX, dtype=jnp.int32)[None, None, :]
    inside = (dest >= entry[..., None]) & (dest <= entry[..., None] + span[..., None])
    counts = jax.random.randint(keys[2], (N_GX, N_GY, N_GX), 1, CAP + 1)
    counts = jnp.where(inside, counts, 0)
    hot_tile = jax.random.randint(keys[3], (N_GY,), 0, N_GX)
    counts = jnp.where(dest == hot_tile[None, :, None], CAP, counts)
    return counts.astype(jnp.int32)


def touch_ends(entries, own_key, least, largest):
    index_at = [jax.random.randint(jax.random.fold_in(own_key, axis), (), 0, length) for axis, length in enumerate(entries.shape)]
    longest = entries.shape.index(max(entries.shape))
    neighbour = index_at[:longest] + [(index_at[longest] + 1) % entries.shape[longest]] + index_at[longest + 1:]
    return entries.at[tuple(index_at)].set(least).at[tuple(neighbour)].set(largest)


def levels(key, extent, cuts, low, high):
    def one(dim, shards_of):
        steps = jax.random.uniform(jax.random.fold_in(jax.random.fold_in(key, 6), dim), (shards_of,), jnp.float32, low / len(cuts), high / len(cuts))
        return jnp.repeat(jnp.exp(steps), extent[dim] // shards_of).reshape((-1,) + (1,) * (len(extent) - dim - 1))

    loudness = one(*cuts[0])
    for cut in cuts[1:]:
        loudness = loudness * one(*cut)
    return loudness


def setup_inputs(seed: int = 0) -> dict:
    seeds = jax.random.split(jax.random.key(seed), 7)
    return {
        "charge_densities": jnp.clip(jnp.exp(math.log(5.0) - 3.218876 * jax.random.uniform(seeds[0], (2, MESH_WIDTH, MESH_HEIGHT, MESH_DEPTH), jnp.float32) ** levels(seeds[0], (2, MESH_WIDTH, MESH_HEIGHT, MESH_DEPTH), ((1, 32), (2, 16)), -0.2, 0.2)), 0.2, 5.0),
        "upwind_linkage": draw_upwind_linkage(jax.random.fold_in(seeds[6], 71), 0),
        "decay_duration": jnp.clip(jnp.exp(math.log(3.0) - 2.3025851 * jax.random.uniform(seeds[2], (MESH_WIDTH, MESH_HEIGHT, MESH_DEPTH), jnp.float32) ** levels(seeds[2], (MESH_WIDTH, MESH_HEIGHT, MESH_DEPTH), ((0, 32), (1, 16)), -0.2, 0.2)), 0.3, 3.0),
        "deposited_packets": jnp.clip(jnp.exp(math.log(4.0) - 2.7725887 * jax.random.uniform(seeds[3], (N_GX, N_GY, N_GX, CAP, ZB), jnp.float32) ** levels(seeds[3], (N_GX, N_GY, N_GX, CAP, ZB), ((0, 32), (1, 16)), -0.2, 0.2)), 0.25, 4.0),
        "active_packet_tally": draw_active_packet_tally(jax.random.fold_in(seeds[6], 71), 0),
        "receiving_packet_position": touch_ends(jax.random.randint(seeds[5], (N_GX, N_GY, N_GX, CAP), 0, BLOCKS), jax.random.fold_in(seeds[5], 1), 0, BLOCKS - 1).astype(jnp.int32),
    }


interval_duration = 0.5
intrinsic_sq = 0.01
trap_level = 0.1


def tridiagonal_solver_routine(values, coupling, axis, backwards):
    moved = jnp.moveaxis(values, axis, 0)
    coef = jnp.moveaxis(coupling, axis, 0)

    def advance(carry, item):
        weight, source = item
        result = (1.0 - weight) * source + weight * carry
        return result, result

    start = jnp.zeros(moved.shape[1:], jnp.float32)
    _, outputs = lax.scan(advance, start, (coef, moved), reverse=backwards)
    return jnp.moveaxis(outputs, 0, axis)


def reference(charge_densities, upwind_linkage, decay_duration, deposited_packets, active_packet_tally, receiving_packet_position):
    density_grid = tridiagonal_solver_routine(charge_densities, upwind_linkage[0], 1, False)
    density_grid = tridiagonal_solver_routine(density_grid, upwind_linkage[0], 1, True)
    density_grid = tridiagonal_solver_routine(density_grid, upwind_linkage[1], 2, False)
    density_grid = tridiagonal_solver_routine(density_grid, upwind_linkage[1], 2, True)
    zblocks = MESH_DEPTH // ZB
    slots = jnp.arange(CAP, dtype=jnp.int32)
    live = (slots[None, None, None, :] < active_packet_tally[..., None]).astype(jnp.float32)
    dest = jnp.arange(N_GX, dtype=jnp.int32)[None, None, :, None]
    row_index = jnp.arange(N_GY, dtype=jnp.int32)[None, :, None, None]
    local_x = receiving_packet_position // (CY * zblocks)
    local_y = (receiving_packet_position // zblocks) % CY
    local_z = receiving_packet_position % zblocks
    segment = ((dest * CX + local_x) * MESH_HEIGHT + row_index * CY + local_y) * zblocks + local_z
    segment = jnp.broadcast_to(segment, receiving_packet_position.shape).astype(jnp.int32)
    values = deposited_packets * live[..., None]
    creation_source = jax.ops.segment_sum(values.reshape(-1, ZB), segment.reshape(-1), num_segments=MESH_WIDTH * MESH_HEIGHT * zblocks)
    creation_source = creation_source.reshape(MESH_WIDTH, MESH_HEIGHT, MESH_DEPTH)
    negative_population = density_grid[0]
    positive_population = density_grid[1]
    spread_coefficient = (negative_population * positive_population - intrinsic_sq) / (decay_duration * (3.0 * (negative_population + trap_level) + (positive_population + trap_level)))
    return density_grid + interval_duration * (creation_source - spread_coefficient)[None]
```

```python
import jax
import jax.numpy as jnp
from jax import lax
from jax.experimental import pallas as pl
from jax.experimental.pallas import tpu as pltpu
from jax.sharding import PartitionSpec as P

MESH = pl.DeviceIdType.MESH
L = 128
interval_duration = 0.5
intrinsic_sq = 0.01
trap_level = 0.1


def kernel(
    c_in, w_in, tau_in, pk_in, cnt_in, site_in, out,
    C, WX, WY, TAU, SITE, CNT,
    psend, seg, xsend, xrecv, rsend, rrecv, esend, ent,
    X, WT, PT, SY, HY, GY, ysend, yrecv, zsend, zrecv,
    smsg, srecv, precv, OUT,
    in_sem, send_sem, recv_sem,
):
    nx = lax.axis_size("gx")
    ny = lax.axis_size("gy")
    nc = nx // 2
    gx = lax.axis_index("gx")
    gy = lax.axis_index("gy")
    q = lax.rem(gx, 2)
    o = 1 - q
    chip = lax.div(gx, 2)
    sub = lax.broadcasted_iota(jnp.int32, (8, L), 0)
    low = sub < 4

    def load(src, dst, i):
        copy = pltpu.make_async_copy(src, dst, in_sem.at[i])
        copy.start()
        return copy

    half = [pl.ds(h * L, L) for h in range(2)]
    first = [load(w_in.at[0, :, half[h]], WX.at[h], h) for h in range(2)]
    first += [load(c_in.at[:, half[h]], C.at[h], 2 + h) for h in range(2)]
    small = [load(site_in, SITE, 4), load(cnt_in, CNT, 5)]
    later = [load(w_in.at[1, :, half[h]], WY.at[h], 6 + h) for h in range(2)]
    last = [load(tau_in.at[:, half[h]], TAU.at[h], 8 + h) for h in range(2)]
    last += [load(pk_in.at[gx], precv.at[gx], 10)]

    barrier = pltpu.get_barrier_semaphore()

    def greet_x(r, z):
        pl.semaphore_signal(
            barrier, inc=1, device_id={"gx": lax.rem(gx + r, nx)}, device_id_type=MESH
        )
        return z

    def greet_y(r, z):
        pl.semaphore_signal(
            barrier, inc=1, device_id={"gy": lax.rem(gy + r, ny)}, device_id_type=MESH
        )
        return z

    lax.fori_loop(1, nx, greet_x, 0)
    lax.fori_loop(1, ny, greet_y, 0)

    def remote(src, dst, i, dev):
        return pltpu.make_async_remote_copy(
            src_ref=src, dst_ref=dst, send_sem=send_sem.at[i], recv_sem=recv_sem.at[i],
            device_id=dev, device_id_type=MESH,
        )

    def take(ref, sem):
        pltpu.make_async_copy(ref, ref, sem).wait()

    for copy in first:
        copy.wait()

    def x_maps(k, dst):
        for h in range(2):
            for t in range(4):
                at = [
                    pl.ds(pl.multiple_of(k * 128 + (x * 32 + t * 8), 8), 8) for x in range(4)
                ]
                w = [WX[h, at[x], :] for x in range(4)]
                c = [C[h, at[x], :] for x in range(4)]
                v = [1.0 - w[x] for x in range(4)]
                f, p = [v[0] * c[0]], [w[0]]
                for x in range(1, 4):
                    f.append(v[x] * c[x] + w[x] * f[-1])
                    p.append(w[x] * p[-1])
                g, e = v[3] * f[3], v[3] * p[3]
                for x in (2, 1, 0):
                    g = v[x] * f[x] + w[x] * g
                    e = v[x] * p[x] + w[x] * e
                for s, val in enumerate((p[3], f[3], e, g)):
                    dst[s, h, pl.ds(t * 8, 8), :] = val

    x_maps(o, psend)
    pl.semaphore_wait(barrier, nx - 1 + ny - 1)
    partner = {"gx": chip * 2 + o}
    pair = remote(psend, seg.at[q], 0, partner)
    pair.start()
    x_maps(q, seg.at[q])
    pair.wait_recv()

    for h in range(2):
        for t in range(4):
            rows = pl.ds(t * 8, 8)
            a0, b0, d0, e0 = [seg[0, s, h, rows, :] for s in range(4)]
            a1, b1, d1, e1 = [seg[1, s, h, rows, :] for s in range(4)]
            a = a0 * a1
            b = a1 * b0 + b1
            d = a0 * a0 * d1 + d0
            e = a0 * (d1 * b0 + e1) + e0
            j = h * 8 + 2 * t
            xsend[j, 0:8, :] = jnp.where(low, a, pltpu.roll(b, 4, 0))
            xsend[j, 8:16, :] = jnp.where(low, d, pltpu.roll(e, 4, 0))
            xsend[j + 1, 0:8, :] = jnp.where(low, pltpu.roll(a, 4, 0), b)
            xsend[j + 1, 8:16, :] = jnp.where(low, pltpu.roll(d, 4, 0), e)

    def send_x(r, z):
        j = lax.rem(chip + r, nc)
        remote(xsend.at[j], xrecv.at[chip], 1, {"gx": j * 2 + q}).start()
        return z

    lax.fori_loop(1, nc, send_x, 0)
    xrecv[chip] = xsend[chip]

    for copy in later:
        copy.wait()
    ya, yd = [], []
    for h in range(2):
        p = None
        for y in range(32):
            w = WY[h, pl.ds(y, 8, stride=32), :]
            WT[h, y] = w
            p = w if p is None else p * w
            PT[h, y] = p
        s = e = None
        for y in range(31, -1, -1):
            w = WT[h, y]
            vp = (1.0 - w) * PT[h, y]
            s = w if s is None else s * w
            e = vp if e is None else vp + w * e
            SY[h, pl.ds(y, 8, stride=32), :] = s
            HY[h, pl.ds(y, 8, stride=32), :] = e
        for r in range(8):
            ysend[2 * r + h, 0:1, :] = s[r : r + 1, :]
            ysend[2 * r + h, 2:3, :] = e[r : r + 1, :]

    for copy in small:
        copy.wait()
    n_dst = SITE.shape[0]
    cap = SITE.shape[1]
    diag = lax.broadcasted_iota(jnp.int32, (n_dst, n_dst), 0) == lax.broadcasted_iota(
        jnp.int32, (n_dst, n_dst), 1
    )
    counts = jnp.broadcast_to(CNT[...].astype(jnp.float32), (n_dst, n_dst))
    live = jnp.sum(jnp.where(diag, counts, 0.0), axis=1, keepdims=True)
    slot = lax.broadcasted_iota(jnp.int32, (n_dst, cap), 1).astype(jnp.float32)
    coded = jnp.where(slot < live, SITE[...].astype(jnp.float32) + 1.0, 0.0)
    lane = lax.broadcasted_iota(jnp.int32, (cap, L), 1)
    place = lax.broadcasted_iota(jnp.int32, (cap, L), 0) + cap * lax.rem(gx, L // cap)
    coded = jnp.dot(
        coded, (lane == place).astype(jnp.float32), preferred_element_type=jnp.float32,
        precision=lax.Precision.HIGHEST,
    )
    for j in range(n_dst):
        smsg[j] = coded[j : j + 1, :]
    srecv[gx] = smsg[gx]

    take(xrecv.at[pl.ds(0, nc - 1)], recv_sem.at[1])
    f = jnp.zeros((4, L), jnp.float32)
    fin = []
    for j in range(nc):
        fin.append(f)
        rsend[j, 0:4, :] = f
        f = xrecv[j, 0:4, :] * f + xrecv[j, 4:8, :]
    b = jnp.zeros((4, L), jnp.float32)
    for j in range(nc - 1, -1, -1):
        rsend[j, 4:8, :] = b
        b = xrecv[j, 0:4, :] * b + (xrecv[j, 8:12, :] * fin[j] + xrecv[j, 12:16, :])

    def send_r(r, z):
        j = lax.rem(chip + r, nc)
        remote(rsend.at[j], rrecv.at[chip], 2, {"gx": j * 2 + q}).start()
        return z

    lax.fori_loop(1, nc, send_r, 0)
    rrecv[chip] = rsend[chip]

    def send_p(r, z):
        j = lax.rem(gx + r, nx)
        remote(pk_in.at[j], precv.at[gx], 3, {"gx": j}).start()
        remote(smsg.at[j], srecv.at[gx], 4, {"gx": j}).start()
        return z

    lax.fori_loop(1, nx, send_p, 0)

    take(rrecv.at[pl.ds(0, nc - 1)], recv_sem.at[2])
    for h in range(2):
        for t in range(4):
            rows = pl.ds(t * 8, 8)
            j = h * 8 + 2 * t
            u0, u1 = rrecv[j], rrecv[j + 1]
            f = jnp.where(low, u0, pltpu.roll(u1, 4, 0))
            b = jnp.where(low, pltpu.roll(u0, 4, 0), u1)
            fm = seg[0, 0, h, rows, :] * f + seg[0, 1, h, rows, :]
            bm = (
                seg[1, 0, h, rows, :] * b + seg[1, 2, h, rows, :] * fm + seg[1, 3, h, rows, :]
            )
            is0 = q == 0
            esend[0, h, rows, :] = jnp.where(is0, fm, f)
            esend[1, h, rows, :] = jnp.where(is0, b, bm)
            ent[q, 0, h, rows, :] = jnp.where(is0, f, fm)
            ent[q, 1, h, rows, :] = jnp.where(is0, bm, b)
    pair2 = remote(esend, ent.at[q], 5, partner)
    pair2.start()

    def x_apply(k):
        for h in range(2):
            for t in range(4):
                rows = pl.ds(t * 8, 8)
                at = [
                    pl.ds(pl.multiple_of(k * 128 + (x * 32 + t * 8), 8), 8) for x in range(4)
                ]
                w = [WX[h, at[x], :] for x in range(4)]
                v = [1.0 - w[x] for x in range(4)]
                f = ent[k, 0, h, rows, :]
                b = ent[k, 1, h, rows, :]
                fs = []
                for x in range(4):
                    f = v[x] * C[h, at[x], :] + w[x] * f
                    fs.append(f)
                for x in (3, 2, 1, 0):
                    b = v[x] * fs[x] + w[x] * b
                    X[h, at[x], :] = b

    x_apply(q)
    pair2.wait_recv()
    x_apply(o)

    for h in range(2):
        f = None
        fs = []
        for y in range(32):
            w = WT[h, y]
            vx = (1.0 - w) * X[h, pl.ds(y, 8, stride=32), :]
            f = vx if f is None else vx + w * f
            PT[h, y] = f
        for r in range(8):
            ysend[2 * r + h, 1:2, :] = f[r : r + 1, :]
        g = None
        for y in range(31, -1, -1):
            w = WT[h, y]
            vf = (1.0 - w) * PT[h, y]
            g = vf if g is None else vf + w * g
            GY[h, pl.ds(y, 8, stride=32), :] = g
        for r in range(8):
            ysend[2 * r + h, 3:4, :] = g[r : r + 1, :]

    def send_y(r, z):
        j = lax.rem(gy + r, ny)
        remote(ysend.at[j], yrecv.at[gy], 6, {"gy": j}).start()
        return z

    lax.fori_loop(1, ny, send_y, 0)
    yrecv[gy] = ysend[gy]
    take(yrecv.at[pl.ds(0, ny - 1)], recv_sem.at[6])

    f = jnp.zeros((1, L), jnp.float32)
    fin = []
    for j in range(ny):
        fin.append(f)
        zsend[j, 0:1, :] = f
        f = yrecv[j, 0:1, :] * f + yrecv[j, 1:2, :]
    b = jnp.zeros((1, L), jnp.float32)
    for j in range(ny - 1, -1, -1):
        zsend[j, 1:2, :] = b
        b = yrecv[j, 0:1, :] * b + (yrecv[j, 2:3, :] * fin[j] + yrecv[j, 3:4, :])

    def send_z(r, z):
        j = lax.rem(gy + r, ny)
        remote(zsend.at[j], zrecv.at[gy], 7, {"gy": j}).start()
        return z

    lax.fori_loop(1, ny, send_z, 0)
    zrecv[gy] = zsend[gy]

    for copy in last:
        copy.wait()
    take(srecv.at[pl.ds(0, nx - 1)], recv_sem.at[4])
    take(precv.at[pl.ds(0, nx - 1)], recv_sem.at[3])
    row = lax.broadcasted_iota(jnp.int32, (2 * L, L), 0)
    code = (2 * lax.rem(row, L) + lax.div(row, L) + 1).astype(jnp.float32)
    gen = None
    per = L // cap
    for m in range(nx // per):
        sites = srecv[m * per]
        for j in range(m * per + 1, (m + 1) * per):
            sites = sites + srecv[j]
        onehot = (code == sites).astype(jnp.float32)
        blocks = precv[m * per : (m + 1) * per].reshape(L, L)
        part = jnp.dot(
            onehot, blocks, preferred_element_type=jnp.float32, precision=lax.Precision.HIGHEST
        )
        gen = part if gen is None else gen + part

    take(zrecv.at[pl.ds(0, ny - 1)], recv_sem.at[7])
    for h in range(2):
        for x in range(4):
            z0, z1 = 2 * x + h, 2 * (4 + x) + h
            fn = jnp.broadcast_to(zrecv[z0, 0:1, :], (8, L))
            bn = jnp.broadcast_to(zrecv[z0, 1:2, :], (8, L))
            fp = jnp.broadcast_to(zrecv[z1, 0:1, :], (8, L))
            bp = jnp.broadcast_to(zrecv[z1, 1:2, :], (8, L))
            for t in range(4):
                i0 = pl.ds(x * 32 + t * 8, 8)
                i1 = pl.ds(128 + x * 32 + t * 8, 8)
                n = GY[h, i0, :] + HY[h, i0, :] * fn + SY[h, i0, :] * bn
                p = GY[h, i1, :] + HY[h, i1, :] * fp + SY[h, i1, :] * bp
                rate = (n * p - intrinsic_sq) / (
                    TAU[h, i0, :] * (3.0 * (n + trap_level) + (p + trap_level))
                )
                k0 = h * L + x * 32 + t * 8
                net = interval_duration * (gen[k0 : k0 + 8, :] - rate)
                OUT[h, i0, :] = n + net
                OUT[h, i1, :] = p + net
    outs = [
        pltpu.make_async_copy(OUT.at[h], out.at[:, half[h]], in_sem.at[11 + h]) for h in range(2)
    ]
    for copy in outs:
        copy.start()
    pair.wait_send()
    take(xsend.at[pl.ds(0, nc - 1)], send_sem.at[1])
    take(rsend.at[pl.ds(0, nc - 1)], send_sem.at[2])
    take(precv.at[pl.ds(0, nx - 1)], send_sem.at[3])
    take(smsg.at[pl.ds(0, nx - 1)], send_sem.at[4])
    pair2.wait_send()
    take(ysend.at[pl.ds(0, ny - 1)], send_sem.at[6])
    take(zsend.at[pl.ds(0, ny - 1)], send_sem.at[7])
    for copy in outs:
        copy.wait()


def on_device(c, w, tau, packets, tally, position):
    f32 = jnp.float32
    nx = packets.shape[2]
    cap = packets.shape[3]
    nc, ny = nx // 2, lax.axis_size("gy")
    v = lambda *s: pltpu.VMEM(s, f32)
    full = (2, 256, L)
    scratch = [
        v(*full), v(*full), v(*full), v(2, 128, L),
        pltpu.VMEM((nx, cap), jnp.int32), pltpu.VMEM((1, nx), jnp.int32),
        v(4, 2, 32, L), v(2, 4, 2, 32, L), v(nc, 16, L), v(nc, 16, L),
        v(nc, 8, L), v(nc, 8, L), v(2, 2, 32, L), v(2, 2, 2, 32, L),
        v(*full), v(2, 32, 8, L), v(2, 32, 8, L), v(*full), v(*full), v(*full),
        v(ny, 4, L), v(ny, 4, L), v(ny, 2, L), v(ny, 2, L),
        v(nx, 1, L), v(nx, 1, L), v(nx, cap, L), v(*full),
        pltpu.SemaphoreType.DMA((13,)),
        pltpu.SemaphoreType.DMA((8,)),
        pltpu.SemaphoreType.DMA((8,)),
    ]
    out = pl.pallas_call(
        kernel,
        out_shape=jax.ShapeDtypeStruct((256, 256), f32),
        in_specs=[pl.BlockSpec(memory_space=pl.ANY)] * 6,
        out_specs=pl.BlockSpec(memory_space=pl.ANY),
        scratch_shapes=scratch,
        compiler_params=pltpu.CompilerParams(
            collective_id=0, has_side_effects=True, vmem_limit_bytes=24 * 1024 * 1024
        ),
        cost_estimate=pl.CostEstimate(
            flops=40_000_000, bytes_accessed=1_500_000, transcendentals=0
        ),
        name="step",
    )(
        c.reshape(256, 256), w.reshape(2, 256, 256), tau.reshape(128, 256),
        packets.reshape(nx, cap, L), tally.reshape(1, nx), position.reshape(nx, cap),
    )
    return out.reshape(c.shape)


def solution(mesh):
    in_specs = (
        P(None, "gx", "gy", None),
        P(None, None, "gx", "gy", None),
        P("gx", "gy", None),
        P("gx", "gy", None, None, None),
        P("gx", "gy", None),
        P("gx", "gy", None, None),
    )
    return jax.shard_map(
        on_device, mesh=mesh, in_specs=in_specs, out_specs=P(None, "gx", "gy", None),
        check_vma=False,
    )
```

```python
import jax
import jax.numpy as jnp
from jax import lax
from jax.experimental import pallas as pl
from jax.experimental.pallas import tpu as pltpu
from jax.sharding import PartitionSpec as P

MESH = pl.DeviceIdType.MESH
L = 128
interval_duration = 0.5
intrinsic_sq = 0.01
trap_level = 0.1


def kernel(
    c_in, w_in, tau_in, pk_in, cnt_in, site_in, out,
    C, WX, WY, TAU, SITE, CNT,
    psend, seg, xsend, xrecv, rsend, rrecv, esend, ent,
    X, WT, PT, SY, HY, GY, ysend, yrecv, zsend, zrecv,
    srow, spair, smsg, srecv, pbuf, precv,
    in_sem, pair_send, pair_recv, send_sem, recv_sem,
):
    nx = lax.axis_size("gx")
    ny = lax.axis_size("gy")
    nc = nx // 2
    gx = lax.axis_index("gx")
    gy = lax.axis_index("gy")
    q = lax.rem(gx, 2)
    o = 1 - q
    chip = lax.div(gx, 2)
    partner = {"gx": chip * 2 + o}
    sub = lax.broadcasted_iota(jnp.int32, (8, L), 0)
    low = sub < 4
    half = [pl.ds(h * L, L) for h in range(2)]
    far = sorted(range(1, nc), key=lambda r: -min(r, nc - r))
    side = 4
    far_y = sorted(
        range(1, ny),
        key=lambda r: -(min(r // side, ny // side - r // side) + min(r % side, side - r % side)),
    )

    def at_chip(r):
        return lax.rem(chip + r, nc)

    def at_y(r):
        row = lax.rem(lax.div(gy, side) + r // side, ny // side)
        return row * side + lax.rem(lax.rem(gy, side) + r % side, side)

    barrier = pltpu.get_barrier_semaphore()

    def greet(dev):
        pl.semaphore_signal(barrier, inc=1, device_id=dev, device_id_type=MESH)

    def load(src, dst, i):
        copy = pltpu.make_async_copy(src, dst, in_sem.at[i])
        copy.start()
        return copy

    for r in far:
        greet({"gx": at_chip(r) * 2 + q})
    greet(partner)
    first = [load(w_in.at[0, :, half[h]], WX.at[h], h) for h in range(2)]
    first += [load(c_in.at[:, half[h]], C.at[h], 2 + h) for h in range(2)]
    for r in far_y:
        greet({"gy": at_y(r)})
    later = [load(w_in.at[1, :, half[h]], WY.at[h], 4 + h) for h in range(2)]
    small = [load(site_in, SITE, 6), load(cnt_in, CNT, 7)]
    mine = load(pk_in.at[:, q], pbuf.at[:, q], 8)
    last = [load(tau_in.at[:, half[h]], TAU.at[h], 9 + h) for h in range(2)]

    def remote(src, dst, i, dev):
        return pltpu.make_async_remote_copy(
            src_ref=src, dst_ref=dst, send_sem=send_sem.at[i], recv_sem=recv_sem.at[i],
            device_id=dev, device_id_type=MESH,
        )

    def take(ref, sem):
        pltpu.make_async_copy(ref, ref, sem).wait()

    for copy in first:
        copy.wait()

    def x_map(k, m, dst):
        h, t = lax.div(m, 4), lax.rem(m, 4)
        at = [pl.ds(pl.multiple_of(k * 128 + x * 32 + t * 8, 8), 8) for x in range(4)]
        w = [WX[h, at[x], :] for x in range(4)]
        c = [C[h, at[x], :] for x in range(4)]
        v = [1.0 - w[x] for x in range(4)]
        f, p = [v[0] * c[0]], [w[0]]
        for x in range(1, 4):
            f.append(v[x] * c[x] + w[x] * f[-1])
            p.append(w[x] * p[-1])
        g, e = v[3] * f[3], v[3] * p[3]
        for x in (2, 1, 0):
            g = v[x] * f[x] + w[x] * g
            e = v[x] * p[x] + w[x] * e
        for s, val in enumerate((p[3], f[3], e, g)):
            dst[m, s] = val

    n_part = 4
    home = lax.div(chip, n_part)
    parts = [lax.rem(home + r, n_part) for r in (2, 1, 3, 0)]
    for c4 in parts:
        for i in range(2):
            x_map(o, c4 * 2 + i, psend)
    pl.semaphore_wait(barrier, nc - 1 + 1 + ny - 1)
    pairs = []
    for i, c4 in enumerate(parts):
        two = pl.ds(c4 * 2, 2)
        pairs.append(
            pltpu.make_async_remote_copy(
                src_ref=psend.at[two], dst_ref=seg.at[q, two],
                send_sem=pair_send.at[i], recv_sem=pair_recv.at[i],
                device_id=partner, device_id_type=MESH,
            )
        )
        pairs[-1].start()
    for c4 in parts:
        for i in range(2):
            x_map(q, c4 * 2 + i, seg.at[q])

    def send_x(j):
        remote(xsend.at[j], xrecv.at[chip], 1, {"gx": j * 2 + q}).start()

    for n, c4 in enumerate(parts):
        pairs[n].wait_recv()
        for i in range(2):
            m = c4 * 2 + i
            a0, b0, d0, e0 = [seg[0, m, s] for s in range(4)]
            a1, b1, d1, e1 = [seg[1, m, s] for s in range(4)]
            a = a0 * a1
            b = a1 * b0 + b1
            d = a0 * a0 * d1 + d0
            e = a0 * (d1 * b0 + e1) + e0
            j = m * 2
            xsend[j, 0:8, :] = jnp.where(low, a, pltpu.roll(b, 4, 0))
            xsend[j, 8:16, :] = jnp.where(low, d, pltpu.roll(e, 4, 0))
            xsend[j + 1, 0:8, :] = jnp.where(low, pltpu.roll(a, 4, 0), b)
            xsend[j + 1, 8:16, :] = jnp.where(low, pltpu.roll(d, 4, 0), e)
            if n < 3:
                send_x(j)
                send_x(j + 1)
    for r in (2, 1, 3):
        send_x(home * 4 + lax.rem(lax.rem(chip, 4) + r, 4))
    xrecv[chip] = xsend[chip]

    ppair = remote(pk_in.at[:, o], pbuf.at[:, q], 0, partner)
    ppair.start()

    for copy in later:
        copy.wait()
    for h in range(2):
        p = None
        for y in range(32):
            w = WY[h, pl.ds(y, 8, stride=32), :]
            WT[h, y] = w
            p = w if p is None else p * w
            PT[h, y] = p
        s = e = None
        for y in range(31, -1, -1):
            w = WT[h, y]
            vp = (1.0 - w) * PT[h, y]
            s = w if s is None else s * w
            e = vp if e is None else vp + w * e
            SY[h, pl.ds(y, 8, stride=32), :] = s
            HY[h, pl.ds(y, 8, stride=32), :] = e
        for r in range(8):
            ysend[2 * r + h, 0:1, :] = s[r : r + 1, :]
            ysend[2 * r + h, 2:3, :] = e[r : r + 1, :]

    for copy in small:
        copy.wait()
    cap, n_dst = SITE.shape
    slot = lax.broadcasted_iota(jnp.int32, (cap, n_dst), 0)
    coded = jnp.where(slot < CNT[...], SITE[...] + 1, 0).astype(jnp.float32)
    lane = lax.broadcasted_iota(jnp.int32, (cap, L), 1)
    per = L // cap
    place = lax.broadcasted_iota(jnp.int32, (cap, L), 0) + cap * lax.rem(gx, per)
    coded = lax.dot_general(
        coded, (lane == place).astype(jnp.float32), (((0,), (0,)), ((), ())),
        preferred_element_type=jnp.float32, precision=lax.Precision.HIGHEST,
    )
    for j in range(n_dst):
        srow[j % 2, j // 2] = coded[j : j + 1, :]
    sp = remote(srow.at[o], spair, 4, partner)
    sp.start()

    take(xrecv.at[pl.ds(0, nc - 1)], recv_sem.at[1])
    f = jnp.zeros((4, L), jnp.float32)
    fin = []
    for j in range(nc):
        fin.append(f)
        rsend[j, 0:4, :] = f
        f = xrecv[j, 0:4, :] * f + xrecv[j, 4:8, :]
    b = jnp.zeros((4, L), jnp.float32)
    for j in range(nc - 1, -1, -1):
        rsend[j, 4:8, :] = b
        b = xrecv[j, 0:4, :] * b + (xrecv[j, 8:12, :] * fin[j] + xrecv[j, 12:16, :])
    for r in far:
        j = at_chip(r)
        remote(rsend.at[j], rrecv.at[chip], 2, {"gx": j * 2 + q}).start()
    rrecv[chip] = rsend[chip]

    sp.wait_recv()
    for j in range(nc):
        smsg[j] = srow[q, j] + spair[j]
    mine.wait()
    ppair.wait_recv()
    for r in far:
        j = at_chip(r)
        remote(pbuf.at[j], precv.at[chip], 3, {"gx": j * 2 + q}).start()
    for r in far:
        j = at_chip(r)
        remote(smsg.at[j], srecv.at[chip], 8, {"gx": j * 2 + q}).start()
    precv[chip] = pbuf[chip]
    srecv[chip] = smsg[chip]

    take(rrecv.at[pl.ds(0, nc - 1)], recv_sem.at[2])
    is0 = q == 0
    for m in range(8):
        u0, u1 = rrecv[2 * m], rrecv[2 * m + 1]
        f = jnp.where(low, u0, pltpu.roll(u1, 4, 0))
        b = jnp.where(low, pltpu.roll(u0, 4, 0), u1)
        fm = seg[0, m, 0] * f + seg[0, m, 1]
        bm = seg[1, m, 0] * b + seg[1, m, 2] * fm + seg[1, m, 3]
        esend[0, m] = jnp.where(is0, fm, f)
        esend[1, m] = jnp.where(is0, b, bm)
        ent[q, 0, m] = jnp.where(is0, f, fm)
        ent[q, 1, m] = jnp.where(is0, bm, b)
    pair2 = remote(esend, ent.at[q], 5, partner)
    pair2.start()

    def x_apply(k):
        for m in range(8):
            h, t = m // 4, m % 4
            at = [pl.ds(pl.multiple_of(k * 128 + x * 32 + t * 8, 8), 8) for x in range(4)]
            w = [WX[h, at[x], :] for x in range(4)]
            v = [1.0 - w[x] for x in range(4)]
            f = ent[k, 0, m]
            b = ent[k, 1, m]
            fs = []
            for x in range(4):
                f = v[x] * C[h, at[x], :] + w[x] * f
                fs.append(f)
            for x in (3, 2, 1, 0):
                b = v[x] * fs[x] + w[x] * b
                X[h, at[x], :] = b

    x_apply(q)
    pair2.wait_recv()
    x_apply(o)

    for h in range(2):
        f = None
        for y in range(32):
            w = WT[h, y]
            vx = (1.0 - w) * X[h, pl.ds(y, 8, stride=32), :]
            f = vx if f is None else vx + w * f
            PT[h, y] = f
        for r in range(8):
            ysend[2 * r + h, 1:2, :] = f[r : r + 1, :]
        g = None
        for y in range(31, -1, -1):
            w = WT[h, y]
            vf = (1.0 - w) * PT[h, y]
            g = vf if g is None else vf + w * g
            GY[h, pl.ds(y, 8, stride=32), :] = g
        for r in range(8):
            ysend[2 * r + h, 3:4, :] = g[r : r + 1, :]
    for r in far_y:
        j = at_y(r)
        remote(ysend.at[j], yrecv.at[gy], 6, {"gy": j}).start()
    yrecv[gy] = ysend[gy]
    take(yrecv.at[pl.ds(0, ny - 1)], recv_sem.at[6])
    f = jnp.zeros((1, L), jnp.float32)
    fin = []
    for j in range(ny):
        fin.append(f)
        zsend[j, 0:1, :] = f
        f = yrecv[j, 0:1, :] * f + yrecv[j, 1:2, :]
    b = jnp.zeros((1, L), jnp.float32)
    for j in range(ny - 1, -1, -1):
        zsend[j, 1:2, :] = b
        b = yrecv[j, 0:1, :] * b + (yrecv[j, 2:3, :] * fin[j] + yrecv[j, 3:4, :])
    for r in far_y:
        j = at_y(r)
        remote(zsend.at[j], zrecv.at[gy], 7, {"gy": j}).start()
    zrecv[gy] = zsend[gy]

    for copy in last:
        copy.wait()
    take(srecv.at[pl.ds(0, nc - 1)], recv_sem.at[8])
    take(precv.at[pl.ds(0, nc - 1)], recv_sem.at[3])
    row = lax.broadcasted_iota(jnp.int32, (2 * L, L), 0)
    code = (2 * lax.rem(row, L) + lax.div(row, L) + 1).astype(jnp.float32)
    gen = None
    for m in range(2):
        lo, hi = m * nc // 2, (m + 1) * nc // 2
        sites = srecv[lo]
        for j in range(lo + 1, hi):
            sites = sites + srecv[j]
        onehot = (code == sites).astype(jnp.float32)
        blocks = precv[lo:hi].reshape(L, L)
        part = jnp.dot(
            onehot, blocks, preferred_element_type=jnp.float32, precision=lax.Precision.HIGHEST
        )
        gen = part if gen is None else gen + part

    take(zrecv.at[pl.ds(0, ny - 1)], recv_sem.at[7])
    for h in range(2):
        for x in range(4):
            z0, z1 = 2 * x + h, 2 * (4 + x) + h
            fn = jnp.broadcast_to(zrecv[z0, 0:1, :], (8, L))
            bn = jnp.broadcast_to(zrecv[z0, 1:2, :], (8, L))
            fp = jnp.broadcast_to(zrecv[z1, 0:1, :], (8, L))
            bp = jnp.broadcast_to(zrecv[z1, 1:2, :], (8, L))
            for t in range(4):
                i0 = pl.ds(x * 32 + t * 8, 8)
                i1 = pl.ds(128 + x * 32 + t * 8, 8)
                n = GY[h, i0, :] + HY[h, i0, :] * fn + SY[h, i0, :] * bn
                p = GY[h, i1, :] + HY[h, i1, :] * fp + SY[h, i1, :] * bp
                rate = (n * p - intrinsic_sq) / (
                    TAU[h, i0, :] * (3.0 * (n + trap_level) + (p + trap_level))
                )
                k0 = h * L + x * 32 + t * 8
                net = interval_duration * (gen[k0 : k0 + 8, :] - rate)
                out[i0, half[h]] = n + net
                out[i1, half[h]] = p + net

    for pair in pairs:
        pair.wait_send()
    ppair.wait_send()
    sp.wait_send()
    pair2.wait_send()
    take(xsend.at[pl.ds(0, nc - 1)], send_sem.at[1])
    take(rsend.at[pl.ds(0, nc - 1)], send_sem.at[2])
    take(precv.at[pl.ds(0, nc - 1)], send_sem.at[3])
    take(smsg.at[pl.ds(0, nc - 1)], send_sem.at[8])
    take(ysend.at[pl.ds(0, ny - 1)], send_sem.at[6])
    take(zsend.at[pl.ds(0, ny - 1)], send_sem.at[7])


def on_device(c, w, tau, packets, tally, position):
    f32 = jnp.float32
    nx = packets.shape[2]
    cap = packets.shape[3]
    nc, ny = nx // 2, lax.axis_size("gy")
    v = lambda *s: pltpu.VMEM(s, f32)
    full = (2, 256, L)
    scratch = [
        v(*full), v(*full), v(*full), v(2, 128, L),
        pltpu.VMEM((cap, nx), jnp.int32), pltpu.VMEM((1, nx), jnp.int32),
        v(8, 4, 8, L), v(2, 8, 4, 8, L), v(nc, 16, L), v(nc, 16, L),
        v(nc, 8, L), v(nc, 8, L), v(2, 8, 8, L), v(2, 2, 8, 8, L),
        v(*full), v(2, 32, 8, L), v(2, 32, 8, L), v(*full), v(*full), v(*full),
        v(ny, 4, L), v(ny, 4, L), v(ny, 2, L), v(ny, 2, L),
        v(2, nc, 1, L), v(nc, 1, L), v(nc, 1, L), v(nc, 1, L),
        v(nc, 2, cap, L), v(nc, 2, cap, L),
        pltpu.SemaphoreType.DMA((11,)),
        pltpu.SemaphoreType.DMA((4,)),
        pltpu.SemaphoreType.DMA((4,)),
        pltpu.SemaphoreType.DMA((9,)),
        pltpu.SemaphoreType.DMA((9,)),
    ]
    out = pl.pallas_call(
        kernel,
        out_shape=pltpu.VMEM((256, 256), f32),
        in_specs=[pl.BlockSpec(memory_space=pl.ANY)] * 6,
        out_specs=pl.BlockSpec(memory_space=pltpu.VMEM),
        scratch_shapes=scratch,
        compiler_params=pltpu.CompilerParams(
            collective_id=0, has_side_effects=True, vmem_limit_bytes=63 * 1024 * 1024
        ),
        cost_estimate=pl.CostEstimate(
            flops=40_000_000, bytes_accessed=1_500_000, transcendentals=0
        ),
        name="step",
    )(
        c.reshape(256, 256), w.reshape(2, 256, 256), tau.reshape(128, 256),
        packets.reshape(nc, 2, cap, L), tally.reshape(1, nx), jnp.swapaxes(position, 2, 3).reshape(cap, nx),
    )
    return out.reshape(c.shape)


def solution(mesh):
    in_specs = (
        P(None, "gx", "gy", None),
        P(None, None, "gx", "gy", None),
        P("gx", "gy", None),
        P("gx", "gy", None, None, None),
        P("gx", "gy", None),
        P("gx", "gy", None, None),
    )
    return jax.shard_map(
        on_device, mesh=mesh, in_specs=in_specs, out_specs=P(None, "gx", "gy", None),
        check_vma=False,
    )
```

```python
import jax
import jax.numpy as jnp
from jax import lax
from jax.experimental import pallas as pl
from jax.experimental.pallas import tpu as pltpu
from jax.sharding import PartitionSpec as P

MESH = pl.DeviceIdType.MESH
L = 128
interval_duration = 0.5
intrinsic_sq = 0.01
trap_level = 0.1


def kernel(
    c_in, w_in, tau_in, pk_in, cnt_in, site_in, out,
    C, WX, WY, TAU, SITE, CNT,
    psend, seg, xsend, xrecv, rsend, rrecv, WX2, C2,
    X, WT, PT, SY, HY, GY, SR, HR, GR, ysend, yrecv, fb,
    srow, spair, pbuf, precv,
    in_sem, pair_send, pair_recv, send_sem, recv_sem, hand,
):
    nx = lax.axis_size("gx")
    ny = lax.axis_size("gy")
    nc = nx // 2
    gx = lax.axis_index("gx")
    gy = lax.axis_index("gy")
    q = lax.rem(gx, 2)
    o = 1 - q
    chip = lax.div(gx, 2)
    partner = {"gx": chip * 2 + o}
    sub = lax.broadcasted_iota(jnp.int32, (8, L), 0)
    low = sub < 4
    half = [pl.ds(h * L, L) for h in range(2)]
    far = sorted(range(1, nc), key=lambda r: -min(r, nc - r))
    side = 4
    far_y = sorted(
        range(1, ny),
        key=lambda r: -(min(r // side, ny // side - r // side) + min(r % side, side - r % side)),
    )

    def at_chip(r):
        return lax.rem(chip + r, nc)

    def at_y(r):
        row = lax.rem(lax.div(gy, side) + r // side, ny // side)
        return row * side + lax.rem(lax.rem(gy, side) + r % side, side)

    barrier = pltpu.get_barrier_semaphore()

    def greet(dev):
        pl.semaphore_signal(barrier, inc=1, device_id=dev, device_id_type=MESH)

    def load(src, dst, i):
        copy = pltpu.make_async_copy(src, dst, in_sem.at[i])
        copy.start()
        return copy

    for r in far:
        greet({"gx": at_chip(r) * 2})

    @pl.when(q == 0)
    def _():
        greet(partner)

    first = [load(w_in.at[0, :, half[h]], WX.at[h], h) for h in range(2)]
    first += [load(c_in.at[:, half[h]], C.at[h], 2 + h) for h in range(2)]
    for r in far_y:
        greet({"gx": chip * 2, "gy": at_y(r)})

    def signal_partner():
        pl.semaphore_signal(hand, inc=1, device_id=partner, device_id_type=MESH)

    own, other = pl.ds(q * 128, 128), pl.ds(o * 128, 128)
    later = [load(w_in.at[1, own, half[h]], WY.at[h, own], 4 + h) for h in range(2)]
    small = [load(site_in, SITE, 6), load(cnt_in, CNT, 7)]
    mine = load(pk_in.at[:, q], pbuf.at[:, pl.ds(q * 8, 8)], 8)
    last = [load(tau_in.at[:, half[h]], TAU.at[h], 9 + h) for h in range(2)]
    again = [load(w_in.at[0, own], WX2.at[q], 11), load(c_in.at[own], C2.at[q], 12)]

    def remote(src, dst, i, dev):
        return pltpu.make_async_remote_copy(
            src_ref=src, dst_ref=dst, send_sem=send_sem.at[i], recv_sem=recv_sem.at[i],
            device_id=dev, device_id_type=MESH,
        )

    def take(ref, sem):
        pltpu.make_async_copy(ref, ref, sem).wait()

    for copy in first:
        copy.wait()

    def x_map(k, m, dst):
        h, t = lax.div(m, 4), lax.rem(m, 4)
        at = [pl.ds(pl.multiple_of(k * 128 + x * 32 + t * 8, 8), 8) for x in range(4)]
        w = [WX[h, at[x], :] for x in range(4)]
        c = [C[h, at[x], :] for x in range(4)]
        v = [1.0 - w[x] for x in range(4)]
        f, p = [v[0] * c[0]], [w[0]]
        for x in range(1, 4):
            f.append(v[x] * c[x] + w[x] * f[-1])
            p.append(w[x] * p[-1])
        g, e = v[3] * f[3], v[3] * p[3]
        for x in (2, 1, 0):
            g = v[x] * f[x] + w[x] * g
            e = v[x] * p[x] + w[x] * e
        for s, val in enumerate((p[3], f[3], e, g)):
            dst[m, s] = val

    n_part = 4
    home = lax.div(chip, n_part)
    parts = [lax.rem(home + r, n_part) for r in (2, 1, 3, 0)]
    for c4 in parts:
        for i in range(2):
            x_map(o, c4 * 2 + i, psend)
    @pl.when(q == 0)
    def _():
        pl.semaphore_wait(hand, 1)

    @pl.when(q == 1)
    def _():
        pl.semaphore_wait(barrier, 1)
        signal_partner()

    pairs = []
    for i, c4 in enumerate(parts):
        two = pl.ds(c4 * 2, 2)
        pairs.append(
            pltpu.make_async_remote_copy(
                src_ref=psend.at[two], dst_ref=seg.at[q, two],
                send_sem=pair_send.at[i], recv_sem=pair_recv.at[i],
                device_id=partner, device_id_type=MESH,
            )
        )
        pairs[-1].start()
    for c4 in parts:
        for i in range(2):
            x_map(q, c4 * 2 + i, seg.at[q])

    def send_x(j):
        remote(xsend.at[j], xrecv.at[chip], 1, {"gx": j * 2 + q}).start()

    for n, c4 in enumerate(parts):
        pairs[n].wait_recv()
        for i in range(2):
            m = c4 * 2 + i
            a0, b0, d0, e0 = [seg[0, m, s] for s in range(4)]
            a1, b1, d1, e1 = [seg[1, m, s] for s in range(4)]
            a = a0 * a1
            b = a1 * b0 + b1
            d = a0 * a0 * d1 + d0
            e = a0 * (d1 * b0 + e1) + e0
            j = m * 2
            xsend[j, 0:8, :] = jnp.where(low, a, pltpu.roll(b, 4, 0))
            xsend[j, 8:16, :] = jnp.where(low, d, pltpu.roll(e, 4, 0))
            xsend[j + 1, 0:8, :] = jnp.where(low, pltpu.roll(a, 4, 0), b)
            xsend[j + 1, 8:16, :] = jnp.where(low, pltpu.roll(d, 4, 0), e)

    swaps = [remote(w_in.at[1, other, half[h]], WY.at[h, own], 9 + h, partner) for h in range(2)]
    swaps += [
        remote(w_in.at[0, other], WX2.at[q], 11, partner),
        remote(c_in.at[other], C2.at[q], 12, partner),
        remote(pk_in.at[:, o], pbuf.at[:, pl.ds(q * 8, 8)], 0, partner),
    ]
    for swap in swaps:
        swap.start()

    @pl.when(q == 0)
    def _():
        pl.semaphore_wait(barrier, 2 * (nc - 1 + ny - 1))
        signal_partner()

    @pl.when(q == 1)
    def _():
        pl.semaphore_wait(hand, 1)

    for r in far:
        send_x(at_chip(r))
    xrecv[chip] = xsend[chip]

    def y_pack(i, h, u, v):
        ysend[i, 0, h] = jnp.where(low, u, pltpu.roll(v, 4, 0))
        ysend[i, 1, h] = jnp.where(low, pltpu.roll(u, 4, 0), v)

    def y_share(i, sem):
        spot = gy * 2 + q
        for r in far_y:
            j = at_y(r)
            for c in range(2):
                dev = {"gx": chip * 2 + c, "gy": j}
                remote(ysend.at[i, c], yrecv.at[i, spot], sem, dev).start()
        remote(ysend.at[i, o], yrecv.at[i, spot], sem, partner).start()
        yrecv[i, spot] = ysend[i, q]

    for copy in later:
        copy.wait()
    for swap in swaps[:2]:
        swap.wait_recv()
    for h in range(2):
        p = None
        for y in range(32):
            w = WY[h, pl.ds(y, 8, stride=32), :]
            WT[h, y] = w
            p = w if p is None else p * w
            PT[h, y] = p
        s = e = None
        for y in range(31, -1, -1):
            w = WT[h, y]
            vp = (1.0 - w) * PT[h, y]
            s = w if s is None else s * w
            e = vp if e is None else vp + w * e
            SY[h, pl.ds(y, 8, stride=32), :] = s
            HY[h, pl.ds(y, 8, stride=32), :] = e
        y_pack(0, h, s, e)

    hs = [remote(SY.at[:, other], SR, 13, partner), remote(HY.at[:, other], HR, 14, partner)]
    for swap in hs:
        swap.start()
    y_share(0, 7)

    for copy in small:
        copy.wait()
    cap, n_dst = SITE.shape
    slot = lax.broadcasted_iota(jnp.int32, (cap, n_dst), 0)
    coded = jnp.where(slot < CNT[...], SITE[...] + 1, 0).astype(jnp.float32)
    lane = lax.broadcasted_iota(jnp.int32, (cap, L), 1)
    per = L // cap
    place = lax.broadcasted_iota(jnp.int32, (cap, L), 0) + cap * lax.rem(gx, per)
    coded = lax.dot_general(
        coded, (lane == place).astype(jnp.float32), (((0,), (0,)), ((), ())),
        preferred_element_type=jnp.float32, precision=lax.Precision.HIGHEST,
    )
    for j in range(n_dst):
        srow[j % 2, j // 2] = coded[j : j + 1, :]
    sp = remote(srow.at[o], spair, 4, partner)
    sp.start()

    mine.wait()
    swaps[4].wait_recv()
    sp.wait_recv()
    for j in range(nc):
        pbuf[j, 16:17, :] = srow[q, j] + spair[j]
    precv[chip] = pbuf[chip]
    for r in far[8:]:
        j = at_chip(r)
        remote(pbuf.at[j], precv.at[chip], 3, {"gx": j * 2 + q}).start()

    take(xrecv.at[pl.ds(0, nc - 1)], recv_sem.at[1])
    f = jnp.zeros((4, L), jnp.float32)
    fin = []
    for j in range(nc):
        fin.append(f)
        rsend[j, 0:4, :] = f
        f = xrecv[j, 0:4, :] * f + xrecv[j, 4:8, :]
    b = jnp.zeros((4, L), jnp.float32)
    for j in range(nc - 1, -1, -1):
        rsend[j, 4:8, :] = b
        b = xrecv[j, 0:4, :] * b + (xrecv[j, 8:12, :] * fin[j] + xrecv[j, 12:16, :])
    for r in far:
        j = at_chip(r)
        remote(rsend.at[j], rrecv.at[chip], 2, {"gx": j * 2 + q}).start()
    rrecv[chip] = rsend[chip]

    for copy in again:
        copy.wait()
    for swap in swaps[2:4]:
        swap.wait_recv()
    take(rrecv.at[pl.ds(0, nc - 1)], recv_sem.at[2])

    for r in far[:8]:
        j = at_chip(r)
        remote(pbuf.at[j], precv.at[chip], 3, {"gx": j * 2 + q}).start()

    for m in range(8):
        h, t = m // 4, m % 4
        u0, u1 = rrecv[2 * m], rrecv[2 * m + 1]
        f = jnp.where(low, u0, pltpu.roll(u1, 4, 0))
        b = jnp.where(low, pltpu.roll(u0, 4, 0), u1)
        at = [(x // 4, pl.ds((x % 4) * 32 + t * 8, 8), half[h]) for x in range(8)]
        w = [WX2[i] for i in at]
        v = [1.0 - w[x] for x in range(8)]
        fs = []
        for x in range(8):
            f = v[x] * C2[at[x]] + w[x] * f
            fs.append(f)
        for x in range(7, -1, -1):
            b = v[x] * fs[x] + w[x] * b
            X[h, pl.ds(x * 32 + t * 8, 8), :] = b

    for h in range(2):
        f = None
        for y in range(32):
            w = WT[h, y]
            vx = (1.0 - w) * X[h, pl.ds(y, 8, stride=32), :]
            f = vx if f is None else vx + w * f
            PT[h, y] = f
        last_f = f
        g = None
        for y in range(31, -1, -1):
            w = WT[h, y]
            vf = (1.0 - w) * PT[h, y]
            g = vf if g is None else vf + w * g
            GY[h, pl.ds(y, 8, stride=32), :] = g
        y_pack(1, h, last_f, g)
    y_share(1, 6)
    gs = remote(GY.at[:, other], GR, 15, partner)
    gs.start()
    for swap in hs:
        swap.wait_recv()
    take(yrecv.at[0, pl.ds(0, 2 * ny - 1)], recv_sem.at[7])
    take(yrecv.at[1, pl.ds(0, 2 * ny - 1)], recv_sem.at[6])
    for k in range(2):
        for h in range(2):
            f = jnp.zeros((4, L), jnp.float32)
            fin = []
            for j in range(ny):
                fin.append(f)
                fb[j, k, h, 0:4, :] = f
                f = yrecv[0, 2 * j + k, h, 0:4, :] * f + yrecv[1, 2 * j + k, h, 0:4, :]
            b = jnp.zeros((4, L), jnp.float32)
            for j in range(ny - 1, -1, -1):
                fb[j, k, h, 4:8, :] = b
                e = yrecv[0, 2 * j + k, h, 4:8, :] * fin[j] + yrecv[1, 2 * j + k, h, 4:8, :]
                b = yrecv[0, 2 * j + k, h, 0:4, :] * b + e
    gs.wait_recv()
    for copy in last:
        copy.wait()
    take(precv.at[pl.ds(0, nc - 1)], recv_sem.at[3])
    row = lax.broadcasted_iota(jnp.int32, (2 * L, L), 0)
    code = (2 * lax.rem(row, L) + lax.div(row, L) + 1).astype(jnp.float32)
    gen = None
    for m in range(2):
        lo, hi = m * nc // 2, (m + 1) * nc // 2
        sites = precv[lo, 16:17, :]
        for j in range(lo + 1, hi):
            sites = sites + precv[j, 16:17, :]
        onehot = (code == sites).astype(jnp.float32)
        blocks = precv[lo:hi, 0:16, :].reshape(L, L)
        part = jnp.dot(
            onehot, blocks, preferred_element_type=jnp.float32, precision=lax.Precision.HIGHEST
        )
        gen = part if gen is None else gen + part

    is0 = q == 0
    for h in range(2):
        for x in range(4):
            f0 = jnp.broadcast_to(fb[gy, q, h, x : x + 1, :], (8, L))
            b0 = jnp.broadcast_to(fb[gy, q, h, 4 + x : 5 + x, :], (8, L))
            f1 = jnp.broadcast_to(fb[gy, o, h, x : x + 1, :], (8, L))
            b1 = jnp.broadcast_to(fb[gy, o, h, 4 + x : 5 + x, :], (8, L))
            for t in range(4):
                i = pl.ds(x * 32 + t * 8, 8)
                i0 = pl.ds(pl.multiple_of(q * 128 + x * 32 + t * 8, 8), 8)
                i1 = pl.ds(pl.multiple_of(o * 128 + x * 32 + t * 8, 8), 8)
                u0 = GY[h, i0, :] + HY[h, i0, :] * f0 + SY[h, i0, :] * b0
                u1 = GR[h, i, :] + HR[h, i, :] * f1 + SR[h, i, :] * b1
                n, p = jnp.where(is0, u0, u1), jnp.where(is0, u1, u0)
                rate = (n * p - intrinsic_sq) / (
                    TAU[h, i, :] * (3.0 * (n + trap_level) + (p + trap_level))
                )
                k0 = h * L + x * 32 + t * 8
                net = interval_duration * (gen[k0 : k0 + 8, :] - rate)
                out[i0, half[h]] = u0 + net
                out[i1, half[h]] = u1 + net

    for copy in pairs + swaps + hs + [sp, gs]:
        copy.wait_send()
    take(xsend.at[pl.ds(0, nc - 1)], send_sem.at[1])
    take(rsend.at[pl.ds(0, nc - 1)], send_sem.at[2])
    take(precv.at[pl.ds(0, nc - 1)], send_sem.at[3])
    take(yrecv.at[0, pl.ds(0, 2 * ny - 1)], send_sem.at[7])
    take(yrecv.at[1, pl.ds(0, 2 * ny - 1)], send_sem.at[6])


def on_device(c, w, tau, packets, tally, position):
    f32 = jnp.float32
    nx = packets.shape[2]
    cap = packets.shape[3]
    nc, ny = nx // 2, lax.axis_size("gy")
    v = lambda *s: pltpu.VMEM(s, f32)
    full = (2, 256, L)
    scratch = [
        v(*full), v(*full), v(*full), v(2, 128, L),
        pltpu.VMEM((cap, nx), jnp.int32), pltpu.VMEM((1, nx), jnp.int32),
        v(8, 4, 8, L), v(2, 8, 4, 8, L), v(nc, 16, L), v(nc, 16, L),
        v(nc, 8, L), v(nc, 8, L), v(2, 128, 256), v(2, 128, 256),
        v(*full), v(2, 32, 8, L), v(2, 32, 8, L), v(*full), v(*full), v(*full),
        v(2, 128, L), v(2, 128, L), v(2, 128, L),
        v(2, 2, 2, 8, L), v(2, 2 * ny, 2, 8, L), v(ny, 2, 2, 8, L),
        v(2, nc, 1, L), v(nc, 1, L),
        v(nc, 2 * cap + 1, L), v(nc, 2 * cap + 1, L),
        pltpu.SemaphoreType.DMA((13,)),
        pltpu.SemaphoreType.DMA((4,)),
        pltpu.SemaphoreType.DMA((4,)),
        pltpu.SemaphoreType.DMA((16,)),
        pltpu.SemaphoreType.DMA((16,)),
        pltpu.SemaphoreType.REGULAR,
    ]
    out = pl.pallas_call(
        kernel,
        out_shape=pltpu.VMEM((256, 256), f32),
        in_specs=[pl.BlockSpec(memory_space=pl.ANY)] * 6,
        out_specs=pl.BlockSpec(memory_space=pltpu.VMEM),
        scratch_shapes=scratch,
        compiler_params=pltpu.CompilerParams(
            collective_id=0, has_side_effects=True, vmem_limit_bytes=63 * 1024 * 1024
        ),
        cost_estimate=pl.CostEstimate(
            flops=40_000_000, bytes_accessed=1_500_000, transcendentals=0
        ),
        name="step",
    )(
        c.reshape(256, 256), w.reshape(2, 256, 256), tau.reshape(128, 256),
        packets.reshape(nc, 2, cap, L), tally.reshape(1, nx), jnp.swapaxes(position, 2, 3).reshape(cap, nx),
    )
    return out.reshape(c.shape)


def solution(mesh):
    in_specs = (
        P(None, "gx", "gy", None),
        P(None, None, "gx", "gy", None),
        P("gx", "gy", None),
        P("gx", "gy", None, None, None),
        P("gx", "gy", None),
        P("gx", "gy", None, None),
    )
    return jax.shard_map(
        on_device, mesh=mesh, in_specs=in_specs, out_specs=P(None, "gx", "gy", None),
        check_vma=False,
    )
```

```python
import jax
import jax.numpy as jnp
from jax import lax
from jax.experimental import pallas as pl
from jax.experimental.pallas import tpu as pltpu
from jax.sharding import PartitionSpec as P

MESH = pl.DeviceIdType.MESH
L = 128
interval_duration = 0.5
intrinsic_sq = 0.01
trap_level = 0.1


def kernel(
    c_in, w_in, tau_in, pk_in, cnt_in, site_in, out,
    C, WX, WY, TAU, SITE, CNT,
    psend, seg, xsend, xrecv, rsend, rrecv, WX2, C2,
    X, WT, PT, SY, HY, GY, SR, HR, GR, ysend, yrecv, fb,
    srow, spair, pbuf, precv,
    in_sem, pair_send, pair_recv, send_sem, recv_sem, hand,
):
    nx = lax.axis_size("gx")
    ny = lax.axis_size("gy")
    nc = nx // 2
    gx = lax.axis_index("gx")
    gy = lax.axis_index("gy")
    q = lax.rem(gx, 2)
    o = 1 - q
    chip = lax.div(gx, 2)
    partner = {"gx": chip * 2 + o}
    sub = lax.broadcasted_iota(jnp.int32, (8, L), 0)
    low = sub < 4
    half = [pl.ds(h * L, L) for h in range(2)]
    far = sorted(range(1, nc), key=lambda r: -min(r, nc - r))
    side = 4
    far_y = sorted(
        range(1, ny),
        key=lambda r: -(min(r // side, ny // side - r // side) + min(r % side, side - r % side)),
    )

    def at_chip(r):
        return lax.rem(chip + r, nc)

    def at_y(r):
        row = lax.rem(lax.div(gy, side) + r // side, ny // side)
        return row * side + lax.rem(lax.rem(gy, side) + r % side, side)

    barrier = pltpu.get_barrier_semaphore()

    def greet(dev):
        pl.semaphore_signal(barrier, inc=1, device_id=dev, device_id_type=MESH)

    def load(src, dst, i):
        copy = pltpu.make_async_copy(src, dst, in_sem.at[i])
        copy.start()
        return copy

    for r in far:
        greet({"gx": at_chip(r) * 2})

    @pl.when(q == 0)
    def _():
        greet(partner)

    first = [load(w_in.at[0, :, half[h]], WX.at[h], h) for h in range(2)]
    first += [load(c_in.at[:, half[h]], C.at[h], 2 + h) for h in range(2)]
    for r in far_y:
        greet({"gx": chip * 2, "gy": at_y(r)})

    def signal_partner():
        pl.semaphore_signal(hand, inc=1, device_id=partner, device_id_type=MESH)

    own, other = pl.ds(q * 128, 128), pl.ds(o * 128, 128)
    later = [load(w_in.at[1, own, half[h]], WY.at[h, own], 4 + h) for h in range(2)]
    small = [load(site_in, SITE, 6), load(cnt_in, CNT, 7)]
    mine = load(pk_in.at[:, q], pbuf.at[:, pl.ds(q * 8, 8)], 8)
    last = [load(tau_in.at[:, half[h]], TAU.at[h], 9 + h) for h in range(2)]
    again = [load(w_in.at[0, own], WX2.at[q], 11), load(c_in.at[own], C2.at[q], 12)]

    def remote(src, dst, i, dev):
        return pltpu.make_async_remote_copy(
            src_ref=src, dst_ref=dst, send_sem=send_sem.at[i], recv_sem=recv_sem.at[i],
            device_id=dev, device_id_type=MESH,
        )

    def take(ref, sem):
        pltpu.make_async_copy(ref, ref, sem).wait()

    for copy in first:
        copy.wait()

    def x_map(k, m, dst):
        h, t = lax.div(m, 4), lax.rem(m, 4)
        at = [pl.ds(pl.multiple_of(k * 128 + x * 32 + t * 8, 8), 8) for x in range(4)]
        w = [WX[h, at[x], :] for x in range(4)]
        c = [C[h, at[x], :] for x in range(4)]
        v = [1.0 - w[x] for x in range(4)]
        f, p = [v[0] * c[0]], [w[0]]
        for x in range(1, 4):
            f.append(v[x] * c[x] + w[x] * f[-1])
            p.append(w[x] * p[-1])
        g, e = v[3] * f[3], v[3] * p[3]
        for x in (2, 1, 0):
            g = v[x] * f[x] + w[x] * g
            e = v[x] * p[x] + w[x] * e
        for s, val in enumerate((p[3], f[3], e, g)):
            dst[m, s] = val

    n_part = 4
    home = lax.div(chip, n_part)
    parts = [lax.rem(home + r, n_part) for r in (2, 1, 3, 0)]
    for c4 in parts:
        for i in range(2):
            x_map(o, c4 * 2 + i, psend)
    @pl.when(q == 0)
    def _():
        pl.semaphore_wait(hand, 1)

    @pl.when(q == 1)
    def _():
        pl.semaphore_wait(barrier, 1)
        signal_partner()

    pairs = []
    for i, c4 in enumerate(parts):
        two = pl.ds(c4 * 2, 2)
        pairs.append(
            pltpu.make_async_remote_copy(
                src_ref=psend.at[two], dst_ref=seg.at[q, two],
                send_sem=pair_send.at[i], recv_sem=pair_recv.at[i],
                device_id=partner, device_id_type=MESH,
            )
        )
        pairs[-1].start()
    for c4 in parts:
        for i in range(2):
            x_map(q, c4 * 2 + i, seg.at[q])

    def send_x(j):
        remote(xsend.at[j], xrecv.at[chip], 1, {"gx": j * 2 + q}).start()

    for n, c4 in enumerate(parts):
        pairs[n].wait_recv()
        for i in range(2):
            m = c4 * 2 + i
            a0, b0, d0, e0 = [seg[0, m, s] for s in range(4)]
            a1, b1, d1, e1 = [seg[1, m, s] for s in range(4)]
            a = a0 * a1
            b = a1 * b0 + b1
            d = a0 * a0 * d1 + d0
            e = a0 * (d1 * b0 + e1) + e0
            j = m * 2
            xsend[j, 0:8, :] = jnp.where(low, a, pltpu.roll(b, 4, 0))
            xsend[j, 8:16, :] = jnp.where(low, d, pltpu.roll(e, 4, 0))
            xsend[j + 1, 0:8, :] = jnp.where(low, pltpu.roll(a, 4, 0), b)
            xsend[j + 1, 8:16, :] = jnp.where(low, pltpu.roll(d, 4, 0), e)

    swaps = [remote(w_in.at[1, other, half[h]], WY.at[h, own], 9 + h, partner) for h in range(2)]
    swaps += [
        remote(w_in.at[0, other], WX2.at[q], 11, partner),
        remote(c_in.at[other], C2.at[q], 12, partner),
        remote(pk_in.at[:, o], pbuf.at[:, pl.ds(q * 8, 8)], 0, partner),
    ]
    for swap in swaps:
        swap.start()

    @pl.when(q == 0)
    def _():
        pl.semaphore_wait(barrier, 2 * (nc - 1 + ny - 1))
        signal_partner()

    @pl.when(q == 1)
    def _():
        pl.semaphore_wait(hand, 1)

    for r in far:
        send_x(at_chip(r))
    xrecv[chip] = xsend[chip]

    def y_pack(i, h, u, v):
        ysend[i, 0, h] = jnp.where(low, u, pltpu.roll(v, 4, 0))
        ysend[i, 1, h] = jnp.where(low, pltpu.roll(u, 4, 0), v)

    def y_share(i, sem):
        spot = gy * 2 + q
        for r in far_y:
            j = at_y(r)
            for c in range(2):
                dev = {"gx": chip * 2 + c, "gy": j}
                remote(ysend.at[i, c], yrecv.at[i, spot], sem, dev).start()
        remote(ysend.at[i, o], yrecv.at[i, spot], sem, partner).start()
        yrecv[i, spot] = ysend[i, q]

    for copy in later:
        copy.wait()
    for swap in swaps[:2]:
        swap.wait_recv()
    for h in range(2):
        p = None
        for y in range(32):
            w = WY[h, pl.ds(y, 8, stride=32), :]
            WT[h, y] = w
            p = w if p is None else p * w
            PT[h, y] = p
        s = e = None
        for y in range(31, -1, -1):
            w = WT[h, y]
            vp = (1.0 - w) * PT[h, y]
            s = w if s is None else s * w
            e = vp if e is None else vp + w * e
            SY[h, pl.ds(y, 8, stride=32), :] = s
            HY[h, pl.ds(y, 8, stride=32), :] = e
        y_pack(0, h, s, e)

    hs = [remote(SY.at[:, other], SR, 13, partner), remote(HY.at[:, other], HR, 14, partner)]
    for swap in hs:
        swap.start()
    y_share(0, 7)

    for copy in small:
        copy.wait()
    cap, n_dst = SITE.shape
    slot = lax.broadcasted_iota(jnp.int32, (cap, n_dst), 0)
    coded = jnp.where(slot < CNT[...], SITE[...] + 1, 0).astype(jnp.float32)
    lane = lax.broadcasted_iota(jnp.int32, (cap, L), 1)
    per = L // cap
    place = lax.broadcasted_iota(jnp.int32, (cap, L), 0) + cap * lax.rem(gx, per)
    coded = lax.dot_general(
        coded, (lane == place).astype(jnp.float32), (((0,), (0,)), ((), ())),
        preferred_element_type=jnp.float32, precision=lax.Precision.HIGHEST,
    )
    for j in range(n_dst):
        srow[j % 2, j // 2] = coded[j : j + 1, :]
    sp = remote(srow.at[o], spair, 4, partner)
    sp.start()

    mine.wait()
    swaps[4].wait_recv()
    sp.wait_recv()
    for j in range(nc):
        pbuf[j, 16:17, :] = srow[q, j] + spair[j]
    precv[chip] = pbuf[chip]
    for r in far[8:]:
        j = at_chip(r)
        remote(pbuf.at[j], precv.at[chip], 3, {"gx": j * 2 + q}).start()

    take(xrecv.at[pl.ds(0, nc - 1)], recv_sem.at[1])
    f = jnp.zeros((4, L), jnp.float32)
    fin = []
    for j in range(nc):
        fin.append(f)
        rsend[j, 0:4, :] = f
        f = xrecv[j, 0:4, :] * f + xrecv[j, 4:8, :]
    b = jnp.zeros((4, L), jnp.float32)
    for j in range(nc - 1, -1, -1):
        rsend[j, 4:8, :] = b
        b = xrecv[j, 0:4, :] * b + (xrecv[j, 8:12, :] * fin[j] + xrecv[j, 12:16, :])
    for r in far:
        j = at_chip(r)
        remote(rsend.at[j], rrecv.at[chip], 2, {"gx": j * 2 + q}).start()
    rrecv[chip] = rsend[chip]

    for copy in again:
        copy.wait()
    for swap in swaps[2:4]:
        swap.wait_recv()
    take(rrecv.at[pl.ds(0, nc - 1)], recv_sem.at[2])

    for m in range(8):
        h, t = m // 4, m % 4
        u0, u1 = rrecv[2 * m], rrecv[2 * m + 1]
        f = jnp.where(low, u0, pltpu.roll(u1, 4, 0))
        b = jnp.where(low, pltpu.roll(u0, 4, 0), u1)
        at = [(x // 4, pl.ds((x % 4) * 32 + t * 8, 8), half[h]) for x in range(8)]
        w = [WX2[i] for i in at]
        v = [1.0 - w[x] for x in range(8)]
        fs = []
        for x in range(8):
            f = v[x] * C2[at[x]] + w[x] * f
            fs.append(f)
        for x in range(7, -1, -1):
            b = v[x] * fs[x] + w[x] * b
            X[h, pl.ds(x * 32 + t * 8, 8), :] = b

    for h in range(2):
        f = None
        for y in range(32):
            w = WT[h, y]
            vx = (1.0 - w) * X[h, pl.ds(y, 8, stride=32), :]
            f = vx if f is None else vx + w * f
            PT[h, y] = f
        last_f = f
        g = None
        for y in range(31, -1, -1):
            w = WT[h, y]
            vf = (1.0 - w) * PT[h, y]
            g = vf if g is None else vf + w * g
            GY[h, pl.ds(y, 8, stride=32), :] = g
        y_pack(1, h, last_f, g)
    y_share(1, 6)
    for r in far[:8]:
        j = at_chip(r)
        remote(pbuf.at[j], precv.at[chip], 3, {"gx": j * 2 + q}).start()

    gs = remote(GY.at[:, other], GR, 15, partner)
    gs.start()
    for swap in hs:
        swap.wait_recv()
    take(yrecv.at[0, pl.ds(0, 2 * ny - 1)], recv_sem.at[7])
    take(yrecv.at[1, pl.ds(0, 2 * ny - 1)], recv_sem.at[6])
    for k in range(2):
        for h in range(2):
            f = jnp.zeros((4, L), jnp.float32)
            fin = []
            for j in range(ny):
                fin.append(f)
                fb[j, k, h, 0:4, :] = f
                f = yrecv[0, 2 * j + k, h, 0:4, :] * f + yrecv[1, 2 * j + k, h, 0:4, :]
            b = jnp.zeros((4, L), jnp.float32)
            for j in range(ny - 1, -1, -1):
                fb[j, k, h, 4:8, :] = b
                e = yrecv[0, 2 * j + k, h, 4:8, :] * fin[j] + yrecv[1, 2 * j + k, h, 4:8, :]
                b = yrecv[0, 2 * j + k, h, 0:4, :] * b + e
    gs.wait_recv()
    for copy in last:
        copy.wait()
    take(precv.at[pl.ds(0, nc - 1)], recv_sem.at[3])
    row = lax.broadcasted_iota(jnp.int32, (2 * L, L), 0)
    code = (2 * lax.rem(row, L) + lax.div(row, L) + 1).astype(jnp.float32)
    gen = None
    for m in range(2):
        lo, hi = m * nc // 2, (m + 1) * nc // 2
        sites = precv[lo, 16:17, :]
        for j in range(lo + 1, hi):
            sites = sites + precv[j, 16:17, :]
        onehot = (code == sites).astype(jnp.float32)
        blocks = precv[lo:hi, 0:16, :].reshape(L, L)
        part = jnp.dot(
            onehot, blocks, preferred_element_type=jnp.float32, precision=lax.Precision.HIGHEST
        )
        gen = part if gen is None else gen + part

    is0 = q == 0
    for h in range(2):
        for x in range(4):
            f0 = jnp.broadcast_to(fb[gy, q, h, x : x + 1, :], (8, L))
            b0 = jnp.broadcast_to(fb[gy, q, h, 4 + x : 5 + x, :], (8, L))
            f1 = jnp.broadcast_to(fb[gy, o, h, x : x + 1, :], (8, L))
            b1 = jnp.broadcast_to(fb[gy, o, h, 4 + x : 5 + x, :], (8, L))
            for t in range(4):
                i = pl.ds(x * 32 + t * 8, 8)
                i0 = pl.ds(pl.multiple_of(q * 128 + x * 32 + t * 8, 8), 8)
                i1 = pl.ds(pl.multiple_of(o * 128 + x * 32 + t * 8, 8), 8)
                u0 = GY[h, i0, :] + HY[h, i0, :] * f0 + SY[h, i0, :] * b0
                u1 = GR[h, i, :] + HR[h, i, :] * f1 + SR[h, i, :] * b1
                n, p = jnp.where(is0, u0, u1), jnp.where(is0, u1, u0)
                rate = (n * p - intrinsic_sq) / (
                    TAU[h, i, :] * (3.0 * (n + trap_level) + (p + trap_level))
                )
                k0 = h * L + x * 32 + t * 8
                net = interval_duration * (gen[k0 : k0 + 8, :] - rate)
                out[i0, half[h]] = u0 + net
                out[i1, half[h]] = u1 + net

    for copy in pairs + swaps + hs + [sp, gs]:
        copy.wait_send()
    take(xsend.at[pl.ds(0, nc - 1)], send_sem.at[1])
    take(rsend.at[pl.ds(0, nc - 1)], send_sem.at[2])
    take(precv.at[pl.ds(0, nc - 1)], send_sem.at[3])
    take(yrecv.at[0, pl.ds(0, 2 * ny - 1)], send_sem.at[7])
    take(yrecv.at[1, pl.ds(0, 2 * ny - 1)], send_sem.at[6])


def on_device(c, w, tau, packets, tally, position):
    f32 = jnp.float32
    nx = packets.shape[2]
    cap = packets.shape[3]
    nc, ny = nx // 2, lax.axis_size("gy")
    v = lambda *s: pltpu.VMEM(s, f32)
    full = (2, 256, L)
    scratch = [
        v(*full), v(*full), v(*full), v(2, 128, L),
        pltpu.VMEM((cap, nx), jnp.int32), pltpu.VMEM((1, nx), jnp.int32),
        v(8, 4, 8, L), v(2, 8, 4, 8, L), v(nc, 16, L), v(nc, 16, L),
        v(nc, 8, L), v(nc, 8, L), v(2, 128, 256), v(2, 128, 256),
        v(*full), v(2, 32, 8, L), v(2, 32, 8, L), v(*full), v(*full), v(*full),
        v(2, 128, L), v(2, 128, L), v(2, 128, L),
        v(2, 2, 2, 8, L), v(2, 2 * ny, 2, 8, L), v(ny, 2, 2, 8, L),
        v(2, nc, 1, L), v(nc, 1, L),
        v(nc, 2 * cap + 1, L), v(nc, 2 * cap + 1, L),
        pltpu.SemaphoreType.DMA((13,)),
        pltpu.SemaphoreType.DMA((4,)),
        pltpu.SemaphoreType.DMA((4,)),
        pltpu.SemaphoreType.DMA((16,)),
        pltpu.SemaphoreType.DMA((16,)),
        pltpu.SemaphoreType.REGULAR,
    ]
    out = pl.pallas_call(
        kernel,
        out_shape=pltpu.VMEM((256, 256), f32),
        in_specs=[pl.BlockSpec(memory_space=pl.ANY)] * 6,
        out_specs=pl.BlockSpec(memory_space=pltpu.VMEM),
        scratch_shapes=scratch,
        compiler_params=pltpu.CompilerParams(
            collective_id=0, has_side_effects=True, vmem_limit_bytes=63 * 1024 * 1024
        ),
        cost_estimate=pl.CostEstimate(
            flops=40_000_000, bytes_accessed=1_500_000, transcendentals=0
        ),
        name="step",
    )(
        c.reshape(256, 256), w.reshape(2, 256, 256), tau.reshape(128, 256),
        packets.reshape(nc, 2, cap, L), tally.reshape(1, nx), jnp.swapaxes(position, 2, 3).reshape(cap, nx),
    )
    return out.reshape(c.shape)


def solution(mesh):
    in_specs = (
        P(None, "gx", "gy", None),
        P(None, None, "gx", "gy", None),
        P("gx", "gy", None),
        P("gx", "gy", None, None, None),
        P("gx", "gy", None),
        P("gx", "gy", None, None),
    )
    return jax.shard_map(
        on_device, mesh=mesh, in_specs=in_specs, out_specs=P(None, "gx", "gy", None),
        check_vma=False,
    )
```

```python
import jax
import jax.numpy as jnp
from jax import lax
from jax.experimental import pallas as pl
from jax.experimental.pallas import tpu as pltpu
from jax.sharding import PartitionSpec as P

MESH = pl.DeviceIdType.MESH
L = 128
interval_duration = 0.5
intrinsic_sq = 0.01
trap_level = 0.1


def kernel(
    c_in, w_in, tau_in, pk_in, cnt_in, site_in, out,
    C, WX, WY, TAU, SITE, CNT,
    psend, seg, xsend, xrecv, rsend, rrecv, WX2, C2,
    X, WT, PT, SY, HY, GY, SR, HR, GR, ysend, yrecv, fb,
    srow, spair, pbuf, precv,
    in_sem, pair_send, pair_recv, send_sem, recv_sem, hand,
):
    nx = lax.axis_size("gx")
    ny = lax.axis_size("gy")
    nc = nx // 2
    gx = lax.axis_index("gx")
    gy = lax.axis_index("gy")
    q = lax.rem(gx, 2)
    o = 1 - q
    chip = lax.div(gx, 2)
    partner = {"gx": chip * 2 + o}
    sub = lax.broadcasted_iota(jnp.int32, (8, L), 0)
    low = sub < 4
    half = [pl.ds(h * L, L) for h in range(2)]
    far = sorted(range(1, nc), key=lambda r: -min(r, nc - r))
    side = 4
    far_y = sorted(
        range(1, ny),
        key=lambda r: -(min(r // side, ny // side - r // side) + min(r % side, side - r % side)),
    )

    def at_chip(r):
        return lax.rem(chip + r, nc)

    def at_y(r):
        row = lax.rem(lax.div(gy, side) + r // side, ny // side)
        return row * side + lax.rem(lax.rem(gy, side) + r % side, side)

    barrier = pltpu.get_barrier_semaphore()

    def greet(dev):
        pl.semaphore_signal(barrier, inc=1, device_id=dev, device_id_type=MESH)

    def load(src, dst, i):
        copy = pltpu.make_async_copy(src, dst, in_sem.at[i])
        copy.start()
        return copy

    @pl.when(q == 0)
    def _():
        greet(partner)

    for r in far:
        greet({"gx": at_chip(r) * 2})

    first = [load(w_in.at[0, :, half[h]], WX.at[h], h) for h in range(2)]
    first += [load(c_in.at[:, half[h]], C.at[h], 2 + h) for h in range(2)]
    for r in far_y:
        greet({"gx": chip * 2, "gy": at_y(r)})

    def signal_partner():
        pl.semaphore_signal(hand, inc=1, device_id=partner, device_id_type=MESH)

    own, other = pl.ds(q * 128, 128), pl.ds(o * 128, 128)
    later = [load(w_in.at[1, own, half[h]], WY.at[h, own], 4 + h) for h in range(2)]
    small = [load(site_in, SITE, 6), load(cnt_in, CNT, 7)]
    mine = load(pk_in.at[:, q], pbuf.at[:, pl.ds(q * 8, 8)], 8)
    last = [load(tau_in.at[:, half[h]], TAU.at[h], 9 + h) for h in range(2)]
    again = [load(w_in.at[0, own], WX2.at[q], 11), load(c_in.at[own], C2.at[q], 12)]

    def remote(src, dst, i, dev):
        return pltpu.make_async_remote_copy(
            src_ref=src, dst_ref=dst, send_sem=send_sem.at[i], recv_sem=recv_sem.at[i],
            device_id=dev, device_id_type=MESH,
        )

    def take(ref, sem):
        pltpu.make_async_copy(ref, ref, sem).wait()

    for copy in first:
        copy.wait()

    def x_map(k, m, dst):
        h, t = lax.div(m, 4), lax.rem(m, 4)
        at = [pl.ds(pl.multiple_of(k * 128 + x * 32 + t * 8, 8), 8) for x in range(4)]
        w = [WX[h, at[x], :] for x in range(4)]
        c = [C[h, at[x], :] for x in range(4)]
        v = [1.0 - w[x] for x in range(4)]
        f, p = [v[0] * c[0]], [w[0]]
        for x in range(1, 4):
            f.append(v[x] * c[x] + w[x] * f[-1])
            p.append(w[x] * p[-1])
        g, e = v[3] * f[3], v[3] * p[3]
        for x in (2, 1, 0):
            g = v[x] * f[x] + w[x] * g
            e = v[x] * p[x] + w[x] * e
        for s, val in enumerate((p[3], f[3], e, g)):
            dst[m, s] = val

    n_part = 4
    home = lax.div(chip, n_part)
    parts = [lax.rem(home + r, n_part) for r in (2, 1, 3, 0)]
    for c4 in parts:
        for i in range(2):
            x_map(o, c4 * 2 + i, psend)
    @pl.when(q == 0)
    def _():
        pl.semaphore_wait(hand, 1)

    @pl.when(q == 1)
    def _():
        pl.semaphore_wait(barrier, 1)
        signal_partner()

    pairs = []
    for i, c4 in enumerate(parts):
        two = pl.ds(c4 * 2, 2)
        pairs.append(
            pltpu.make_async_remote_copy(
                src_ref=psend.at[two], dst_ref=seg.at[q, two],
                send_sem=pair_send.at[i], recv_sem=pair_recv.at[i],
                device_id=partner, device_id_type=MESH,
            )
        )
        pairs[-1].start()
    for c4 in parts:
        for i in range(2):
            x_map(q, c4 * 2 + i, seg.at[q])

    def send_x(j):
        remote(xsend.at[j], xrecv.at[chip], 1, {"gx": j * 2 + q}).start()

    for n, c4 in enumerate(parts):
        pairs[n].wait_recv()
        for i in range(2):
            m = c4 * 2 + i
            a0, b0, d0, e0 = [seg[0, m, s] for s in range(4)]
            a1, b1, d1, e1 = [seg[1, m, s] for s in range(4)]
            a = a0 * a1
            b = a1 * b0 + b1
            d = a0 * a0 * d1 + d0
            e = a0 * (d1 * b0 + e1) + e0
            j = m * 2
            xsend[j, 0:8, :] = jnp.where(low, a, pltpu.roll(b, 4, 0))
            xsend[j, 8:16, :] = jnp.where(low, d, pltpu.roll(e, 4, 0))
            xsend[j + 1, 0:8, :] = jnp.where(low, pltpu.roll(a, 4, 0), b)
            xsend[j + 1, 8:16, :] = jnp.where(low, pltpu.roll(d, 4, 0), e)

    swaps = [remote(w_in.at[1, other, half[h]], WY.at[h, own], 9 + h, partner) for h in range(2)]
    swaps += [
        remote(w_in.at[0, other], WX2.at[q], 11, partner),
        remote(c_in.at[other], C2.at[q], 12, partner),
        remote(pk_in.at[:, o], pbuf.at[:, pl.ds(q * 8, 8)], 0, partner),
    ]
    for swap in swaps:
        swap.start()

    @pl.when(q == 0)
    def _():
        pl.semaphore_wait(barrier, 2 * (nc - 1 + ny - 1))
        signal_partner()

    @pl.when(q == 1)
    def _():
        pl.semaphore_wait(hand, 1)

    for r in far:
        send_x(at_chip(r))
    xrecv[chip] = xsend[chip]

    def y_pack(i, h, u, v):
        ysend[i, 0, h] = jnp.where(low, u, pltpu.roll(v, 4, 0))
        ysend[i, 1, h] = jnp.where(low, pltpu.roll(u, 4, 0), v)

    def y_share(i, sem):
        spot = gy * 2 + q
        for c in (o, q):
            for r in far_y:
                dev = {"gx": chip * 2 + c, "gy": at_y(r)}
                remote(ysend.at[i, c], yrecv.at[i, spot], sem, dev).start()
        remote(ysend.at[i, o], yrecv.at[i, spot], sem, partner).start()
        yrecv[i, spot] = ysend[i, q]

    for copy in later:
        copy.wait()
    for swap in swaps[:2]:
        swap.wait_recv()
    for h in range(2):
        p = None
        for y in range(32):
            w = WY[h, pl.ds(y, 8, stride=32), :]
            WT[h, y] = w
            p = w if p is None else p * w
            PT[h, y] = p
        s = e = None
        for y in range(31, -1, -1):
            w = WT[h, y]
            vp = (1.0 - w) * PT[h, y]
            s = w if s is None else s * w
            e = vp if e is None else vp + w * e
            SY[h, pl.ds(y, 8, stride=32), :] = s
            HY[h, pl.ds(y, 8, stride=32), :] = e
        y_pack(0, h, s, e)

    hs = [remote(SY.at[:, other], SR, 13, partner), remote(HY.at[:, other], HR, 14, partner)]

    for copy in small:
        copy.wait()
    cap, n_dst = SITE.shape
    slot = lax.broadcasted_iota(jnp.int32, (cap, n_dst), 0)
    coded = jnp.where(slot < CNT[...], SITE[...] + 1, 0).astype(jnp.float32)
    lane = lax.broadcasted_iota(jnp.int32, (cap, L), 1)
    per = L // cap
    place = lax.broadcasted_iota(jnp.int32, (cap, L), 0) + cap * lax.rem(gx, per)
    coded = lax.dot_general(
        coded, (lane == place).astype(jnp.float32), (((0,), (0,)), ((), ())),
        preferred_element_type=jnp.float32, precision=lax.Precision.HIGHEST,
    )
    for j in range(n_dst):
        srow[j % 2, j // 2] = coded[j : j + 1, :]
    sp = remote(srow.at[o], spair, 4, partner)
    sp.start()

    mine.wait()
    swaps[4].wait_recv()
    sp.wait_recv()
    for j in range(nc):
        pbuf[j, 16:17, :] = srow[q, j] + spair[j]
    precv[chip] = pbuf[chip]
    for r in far[8:]:
        j = at_chip(r)
        remote(pbuf.at[j], precv.at[chip], 3, {"gx": j * 2 + q}).start()

    take(xrecv.at[pl.ds(0, nc - 1)], recv_sem.at[1])
    f = jnp.zeros((4, L), jnp.float32)
    fin = []
    for j in range(nc):
        fin.append(f)
        rsend[j, 0:4, :] = f
        f = xrecv[j, 0:4, :] * f + xrecv[j, 4:8, :]
    b = jnp.zeros((4, L), jnp.float32)
    for j in range(nc - 1, -1, -1):
        rsend[j, 4:8, :] = b
        b = xrecv[j, 0:4, :] * b + (xrecv[j, 8:12, :] * fin[j] + xrecv[j, 12:16, :])
    for r in far:
        j = at_chip(r)
        remote(rsend.at[j], rrecv.at[chip], 2, {"gx": j * 2 + q}).start()
    rrecv[chip] = rsend[chip]

    for copy in again:
        copy.wait()
    for swap in swaps[2:4]:
        swap.wait_recv()
    for swap in hs:
        swap.start()
    y_share(0, 7)
    take(rrecv.at[pl.ds(0, nc - 1)], recv_sem.at[2])

    for m in range(8):
        h, t = m // 4, m % 4
        u0, u1 = rrecv[2 * m], rrecv[2 * m + 1]
        f = jnp.where(low, u0, pltpu.roll(u1, 4, 0))
        b = jnp.where(low, pltpu.roll(u0, 4, 0), u1)
        at = [(x // 4, pl.ds((x % 4) * 32 + t * 8, 8), half[h]) for x in range(8)]
        w = [WX2[i] for i in at]
        v = [1.0 - w[x] for x in range(8)]
        fs = []
        for x in range(8):
            f = v[x] * C2[at[x]] + w[x] * f
            fs.append(f)
        for x in range(7, -1, -1):
            b = v[x] * fs[x] + w[x] * b
            X[h, pl.ds(x * 32 + t * 8, 8), :] = b

    for h in range(2):
        f = None
        for y in range(32):
            w = WT[h, y]
            vx = (1.0 - w) * X[h, pl.ds(y, 8, stride=32), :]
            f = vx if f is None else vx + w * f
            PT[h, y] = f
        last_f = f
        g = None
        for y in range(31, -1, -1):
            w = WT[h, y]
            vf = (1.0 - w) * PT[h, y]
            g = vf if g is None else vf + w * g
            GY[h, pl.ds(y, 8, stride=32), :] = g
        y_pack(1, h, last_f, g)
    y_share(1, 6)
    for r in far[:8]:
        j = at_chip(r)
        remote(pbuf.at[j], precv.at[chip], 3, {"gx": j * 2 + q}).start()

    gs = remote(GY.at[:, other], GR, 15, partner)
    gs.start()
    for swap in hs:
        swap.wait_recv()
    take(yrecv.at[0, pl.ds(0, 2 * ny - 1)], recv_sem.at[7])
    take(yrecv.at[1, pl.ds(0, 2 * ny - 1)], recv_sem.at[6])
    for k in range(2):
        for h in range(2):
            f = jnp.zeros((4, L), jnp.float32)
            fin = []
            for j in range(ny):
                fin.append(f)
                fb[j, k, h, 0:4, :] = f
                f = yrecv[0, 2 * j + k, h, 0:4, :] * f + yrecv[1, 2 * j + k, h, 0:4, :]
            b = jnp.zeros((4, L), jnp.float32)
            for j in range(ny - 1, -1, -1):
                fb[j, k, h, 4:8, :] = b
                e = yrecv[0, 2 * j + k, h, 4:8, :] * fin[j] + yrecv[1, 2 * j + k, h, 4:8, :]
                b = yrecv[0, 2 * j + k, h, 0:4, :] * b + e
    gs.wait_recv()
    for copy in last:
        copy.wait()
    take(precv.at[pl.ds(0, nc - 1)], recv_sem.at[3])
    row = lax.broadcasted_iota(jnp.int32, (2 * L, L), 0)
    code = (2 * lax.rem(row, L) + lax.div(row, L) + 1).astype(jnp.float32)
    gen = None
    for m in range(2):
        lo, hi = m * nc // 2, (m + 1) * nc // 2
        sites = precv[lo, 16:17, :]
        for j in range(lo + 1, hi):
            sites = sites + precv[j, 16:17, :]
        onehot = (code == sites).astype(jnp.float32)
        blocks = precv[lo:hi, 0:16, :].reshape(L, L)
        part = jnp.dot(
            onehot, blocks, preferred_element_type=jnp.float32, precision=lax.Precision.HIGHEST
        )
        gen = part if gen is None else gen + part

    is0 = q == 0
    for h in range(2):
        for x in range(4):
            f0 = jnp.broadcast_to(fb[gy, q, h, x : x + 1, :], (8, L))
            b0 = jnp.broadcast_to(fb[gy, q, h, 4 + x : 5 + x, :], (8, L))
            f1 = jnp.broadcast_to(fb[gy, o, h, x : x + 1, :], (8, L))
            b1 = jnp.broadcast_to(fb[gy, o, h, 4 + x : 5 + x, :], (8, L))
            for t in range(4):
                i = pl.ds(x * 32 + t * 8, 8)
                i0 = pl.ds(pl.multiple_of(q * 128 + x * 32 + t * 8, 8), 8)
                i1 = pl.ds(pl.multiple_of(o * 128 + x * 32 + t * 8, 8), 8)
                u0 = GY[h, i0, :] + HY[h, i0, :] * f0 + SY[h, i0, :] * b0
                u1 = GR[h, i, :] + HR[h, i, :] * f1 + SR[h, i, :] * b1
                n, p = jnp.where(is0, u0, u1), jnp.where(is0, u1, u0)
                rate = (n * p - intrinsic_sq) / (
                    TAU[h, i, :] * (3.0 * (n + trap_level) + (p + trap_level))
                )
                k0 = h * L + x * 32 + t * 8
                net = interval_duration * (gen[k0 : k0 + 8, :] - rate)
                out[i0, half[h]] = u0 + net
                out[i1, half[h]] = u1 + net

    for copy in pairs + swaps + hs + [sp, gs]:
        copy.wait_send()
    take(xsend.at[pl.ds(0, nc - 1)], send_sem.at[1])
    take(rsend.at[pl.ds(0, nc - 1)], send_sem.at[2])
    take(precv.at[pl.ds(0, nc - 1)], send_sem.at[3])
    take(yrecv.at[0, pl.ds(0, 2 * ny - 1)], send_sem.at[7])
    take(yrecv.at[1, pl.ds(0, 2 * ny - 1)], send_sem.at[6])


def on_device(c, w, tau, packets, tally, position):
    f32 = jnp.float32
    nx = packets.shape[2]
    cap = packets.shape[3]
    nc, ny = nx // 2, lax.axis_size("gy")
    v = lambda *s: pltpu.VMEM(s, f32)
    full = (2, 256, L)
    scratch = [
        v(*full), v(*full), v(*full), v(2, 128, L),
        pltpu.VMEM((cap, nx), jnp.int32), pltpu.VMEM((1, nx), jnp.int32),
        v(8, 4, 8, L), v(2, 8, 4, 8, L), v(nc, 16, L), v(nc, 16, L),
        v(nc, 8, L), v(nc, 8, L), v(2, 128, 256), v(2, 128, 256),
        v(*full), v(2, 32, 8, L), v(2, 32, 8, L), v(*full), v(*full), v(*full),
        v(2, 128, L), v(2, 128, L), v(2, 128, L),
        v(2, 2, 2, 8, L), v(2, 2 * ny, 2, 8, L), v(ny, 2, 2, 8, L),
        v(2, nc, 1, L), v(nc, 1, L),
        v(nc, 2 * cap + 1, L), v(nc, 2 * cap + 1, L),
        pltpu.SemaphoreType.DMA((13,)),
        pltpu.SemaphoreType.DMA((4,)),
        pltpu.SemaphoreType.DMA((4,)),
        pltpu.SemaphoreType.DMA((16,)),
        pltpu.SemaphoreType.DMA((16,)),
        pltpu.SemaphoreType.REGULAR,
    ]
    out = pl.pallas_call(
        kernel,
        out_shape=pltpu.VMEM((256, 256), f32),
        in_specs=[pl.BlockSpec(memory_space=pl.ANY)] * 6,
        out_specs=pl.BlockSpec(memory_space=pltpu.VMEM),
        scratch_shapes=scratch,
        compiler_params=pltpu.CompilerParams(
            collective_id=0, has_side_effects=True, vmem_limit_bytes=63 * 1024 * 1024
        ),
        cost_estimate=pl.CostEstimate(
            flops=40_000_000, bytes_accessed=1_500_000, transcendentals=0
        ),
        name="step",
    )(
        c.reshape(256, 256), w.reshape(2, 256, 256), tau.reshape(128, 256),
        packets.reshape(nc, 2, cap, L), tally.reshape(1, nx), jnp.swapaxes(position, 2, 3).reshape(cap, nx),
    )
    return out.reshape(c.shape)


def solution(mesh):
    in_specs = (
        P(None, "gx", "gy", None),
        P(None, None, "gx", "gy", None),
        P("gx", "gy", None),
        P("gx", "gy", None, None, None),
        P("gx", "gy", None),
        P("gx", "gy", None, None),
    )
    return jax.shard_map(
        on_device, mesh=mesh, in_specs=in_specs, out_specs=P(None, "gx", "gy", None),
        check_vma=False,
    )
```
